32 devices in a mesh: dp: 8 (over z, x), expert: 4 (over y, core).
Axes of the slice: x: 2, y: 2, z: 4, core: 2. Of those that a mesh axis runs over, the one named last changes fastest.
Arguments:
- tokens: bfloat16 [1024, 4096], P('dp', 'expert'), may hold values from -6 to 6
- expert_ids: int32 [1024, 8], P('dp'), may hold values from 0 to 7, all different within a row; in each aligned block of 128 rows (0 to 127, 128 to 255, ...) at most 128 rows name the same one
- scores: float32 [1024, 8], P('dp'), may hold values from 0.05 to 1
- weight_in: bfloat16 [8, 4096, 2048], P('dp', 'expert'), may hold values from -0.09375 to 0.09375
- weight_out: bfloat16 [8, 1024, 4096], P('dp', None, 'expert'), may hold values from -0.1875 to 0.1875
- out_grad: bfloat16 [1024, 4096], P('dp', 'expert'), may hold values from -6 to 6
Outputs:
- layer_out: bfloat16 [1024, 4096], P('dp', 'expert')
- tokens_grad: bfloat16 [1024, 4096], P('dp', 'expert')
- scores_grad: float32 [1024, 8], P('dp')
- w_in_grad: bfloat16 [8, 4096, 2048], P('dp', 'expert')
- w_out_grad: bfloat16 [8, 1024, 4096], P('dp', None, 'expert')
The draws below stay inside these ranges and needn't reach their ends.
Inputs may be any that keep to these rules, and one draw needn't show every extreme that they name: `expert_ids`: the 8 experts of a token differ. Among the 128 consecutive tokens of one index of dp no expert is named by more than 128 choices, and in every draw some such block names some expert exactly 128 times.
All inputs are finite; a program needn't handle non-finite values.
Results may differ from the reference program's by a relative error of at most 0.0064.
Values may be sent and summed in bfloat16 or wider, within the bound.
A program may use at most 128 MiB of HBM per device.

```python
import math
import jax
import jax.numpy as jnp
import numpy as np
from jax import lax

D = 4096
FF = 1024
TOP = 8
TOK_DEV = 128
EXPERTS = 8
CAP = 128
TOKENS = 1024
N_DP = 8


def block_scale(rng, shape, pieces, smallest, largest):
    factor_of = 1.0
    for dim, blocks in pieces:
        draws = jax.random.uniform(jax.random.fold_in(jax.random.fold_in(rng, 6), dim), (blocks,), jnp.float32, smallest / len(pieces), largest / len(pieces))
        factor_of = factor_of * jnp.repeat(jnp.exp(draws), shape[dim] // blocks).reshape((-1,) + (1,) * (len(shape) - 1 - dim))
    return factor_of


def routed_block(key, own, number, rows, count, top, bound, skew):
    ranking = jax.random.permutation(key, count)
    crowded, common = shares(count, rows * top, bound, skew, True), shares(count, rows * top, bound, skew, False)
    places = jnp.arange(count)

    def named(tallies, rotation):
        used = int((tallies > 0).sum())
        fixed = max(1, used // 4)
        moved = fixed + (places - fixed + rotation * (used - fixed)) % max(1, count - fixed)
        return jnp.zeros((count,), jnp.int32).at[ranking[jnp.where(places < fixed, places, moved)]].set(jnp.asarray(tallies, jnp.int32))

    tallies = jnp.where(number % 4 == 0, named(crowded, number // 4), named(common, number - number // 4 - 1))
    mixed = jax.random.permutation(jax.random.fold_in(own, 3), count)
    giver, receiver = mixed[0:count // 2 * 2:2], mixed[1:count // 2 * 2:2]
    slack = jnp.minimum(tallies[giver] - 1, bound - tallies[receiver]) // 2
    slack = jnp.where((giver == ranking[0]) | (receiver == ranking[0]) | (tallies[receiver] == 0), 0, jnp.maximum(slack, 0))
    moved = jax.random.randint(jax.random.fold_in(own, 4), (count // 2,), 0, 1 << 20) % (slack + 1)
    tallies = tallies.at[giver].add(-moved).at[receiver].add(moved)
    items = jnp.searchsorted(jnp.cumsum(tallies), jnp.arange(rows * top), side="right").astype(jnp.int32)
    listing = items.reshape(top, rows).T
    listing = listing[jax.random.permutation(jax.random.fold_in(own, 1), rows)]
    rotation = jax.random.randint(jax.random.fold_in(own, 2), (rows, 1), 0, top)
    return jnp.take_along_axis(listing, (jnp.arange(top)[None, :] + rotation) % top, axis=1)


def shares(number_of, total, most, lean, full):
    weights = [(1 << 20) // math.isqrt(standing ** lean) + 1 for standing in range(1, number_of + 1)]
    largest = most if full else min(most, max(-(-total // number_of), total * weights[0] // sum(weights)))
    least = 1 if total - largest >= number_of - 1 else 0
    given, rest = [largest] + [least] * (number_of - 1), total - largest - least * (number_of - 1)
    while rest > 0:
        movable = [i for i in range(1, number_of) if given[i] < largest] or [i for i in range(1, number_of) if given[i] < most]
        mass, left = sum([weights[i] for i in movable]), rest
        for i in movable:
            more = min(most - given[i], max(1, left * weights[i] // mass), rest)
            given[i] = given[i] + more
            rest = rest - more
    return np.array(given)


def noise(stream_key, dims, deviation, bound, split=(), kind=jnp.bfloat16):
    values = deviation * jax.random.normal(stream_key, dims, jnp.float32)
    if split:
        values = values * block_scale(stream_key, dims, split, -0.22, 0.18)
    return jnp.clip(values, -bound, bound).astype(kind)


def setup_inputs(seed: int = 0) -> dict:
    seeds = jax.random.split(jax.random.key(seed), 7)
    tokens = noise(seeds[0], (TOKENS, D), 1.0, 6.0, ((0, 8), (1, 4)))
    expert_ids_keys = jax.random.split(jax.random.fold_in(seeds[1], 1), TOKENS // TOK_DEV)
    expert_ids_turns = jax.random.permutation(jax.random.fold_in(seeds[1], 3), TOKENS // TOK_DEV)
    expert_ids = jax.vmap(lambda own, number: routed_block(jax.random.fold_in(seeds[1], 2), own, number, TOK_DEV, EXPERTS, TOP, CAP, 2))(expert_ids_keys, expert_ids_turns).reshape((TOKENS, TOP))
    scores = jnp.clip(jnp.exp(math.log(1.0) - 2.9957323 * jax.random.uniform(seeds[2], (TOKENS, TOP), jnp.float32) ** block_scale(seeds[2], (TOKENS, TOP), ((0, 8),), -0.2, 0.2)), 0.05, 1.0)
    weight_in = noise(seeds[3], (EXPERTS, D, 2 * FF), D ** -0.5, 0.09375, ((0, 8), (1, 4)))
    weight_out = noise(seeds[4], (EXPERTS, FF, D), FF ** -0.5, 0.1875, ((0, 8), (2, 4)))
    out_grad = noise(seeds[5], (TOKENS, D), 1.0, 6.0, ((0, 8), (1, 4)))
    return {"tokens": tokens, "expert_ids": expert_ids, "scores": scores, "weight_in": weight_in, "weight_out": weight_out, "out_grad": out_grad}


ROUTE_SCALE = 2.5


def expert_pass(weight_in_e, weight_out_e, rows_x, rows_grad):
    gate_up = jnp.dot(rows_x, weight_in_e, preferred_element_type=jnp.float32)
    gate = gate_up[:, :FF]
    upward = gate_up[:, FF:]
    sigma = jax.nn.sigmoid(gate)
    hidden = (gate * sigma * upward).astype(jnp.bfloat16)
    expert_out = jnp.dot(hidden, weight_out_e, preferred_element_type=jnp.float32).astype(jnp.bfloat16)
    hidden_grad = jnp.dot(rows_grad, weight_out_e.T, preferred_element_type=jnp.float32)
    gate_up_grad = jnp.concatenate(
        [hidden_grad * upward * sigma * (1.0 + gate * (1.0 - sigma)), hidden_grad * gate * sigma], axis=1
    ).astype(jnp.bfloat16)
    choice_grad = jnp.dot(gate_up_grad, weight_in_e.T, preferred_element_type=jnp.float32).astype(jnp.bfloat16)
    in_weight = jnp.dot(rows_x.T, gate_up_grad, preferred_element_type=jnp.float32).astype(jnp.bfloat16)
    out_weight = jnp.dot(hidden.T, rows_grad, preferred_element_type=jnp.float32).astype(jnp.bfloat16)
    return expert_out, choice_grad, in_weight, out_weight


def reference(tokens, expert_ids, scores, weight_in, weight_out, out_grad):
    blocks = N_DP
    per_block = TOK_DEV * TOP
    routed_all = blocks * per_block
    ids_blocks = expert_ids.reshape(blocks, per_block)
    expert_hot = (ids_blocks[:, :, None] == jnp.arange(EXPERTS, dtype=jnp.int32)[None, None, :]).astype(jnp.int32)
    earlier = jnp.sum((jnp.cumsum(expert_hot, axis=1) - expert_hot) * expert_hot, axis=2)
    position = jnp.arange(blocks, dtype=jnp.int32)[:, None] * CAP + earlier
    routed_index = jnp.arange(routed_all, dtype=jnp.int32).reshape(blocks, per_block)
    table = jnp.full((EXPERTS, blocks * CAP), routed_all, jnp.int32).at[ids_blocks, position].set(routed_index)

    score_total = jnp.sum(scores, axis=1, keepdims=True)
    route_weights = ROUTE_SCALE * scores / score_total
    tokens_pad = jnp.concatenate([tokens, jnp.zeros((1, D), tokens.dtype)], axis=0)
    grad_pad = jnp.concatenate([out_grad.astype(jnp.float32), jnp.zeros((1, D), jnp.float32)], axis=0)
    weight_flat = jnp.concatenate([route_weights.reshape(-1), jnp.zeros((1,), jnp.float32)], axis=0)

    def one_expert(operands):
        weight_in_e, weight_out_e, entries = operands
        owner = entries // TOP
        rows_x = tokens_pad[owner]
        rows_grad = (weight_flat[entries][:, None] * grad_pad[owner]).astype(jnp.bfloat16)
        return expert_pass(weight_in_e, weight_out_e, rows_x, rows_grad)

    expert_out, choice_grad, w_in_grad, w_out_grad = lax.map(one_expert, (weight_in, weight_out, table))
    flat_table = table.reshape(-1)
    out_rows = jnp.zeros((routed_all + 1, D), expert_out.dtype).at[flat_table].set(expert_out.reshape(-1, D))
    grad_rows = jnp.zeros((routed_all + 1, D), choice_grad.dtype).at[flat_table].set(choice_grad.reshape(-1, D))
    picked = out_rows[:routed_all].astype(jnp.float32).reshape(TOKENS, TOP, D)
    layer_out = jnp.sum(route_weights[:, :, None] * picked, axis=1).astype(jnp.bfloat16)
    tokens_grad = jnp.sum(grad_rows[:routed_all].astype(jnp.float32).reshape(TOKENS, TOP, D), axis=1).astype(jnp.bfloat16)
    choice_dot = jnp.sum(out_grad.astype(jnp.float32)[:, None, :] * picked, axis=2)
    scores_grad = (ROUTE_SCALE * choice_dot - jnp.sum(choice_dot * route_weights, axis=1, keepdims=True)) / score_total
    return layer_out, tokens_grad, scores_grad, w_in_grad, w_out_grad
```

```python
import jax
import jax.numpy as jnp
from jax import lax
from jax.sharding import PartitionSpec as P

ROUTE_SCALE = 2.5


def gate_terms(gate_up, hidden_units):
    gate = gate_up[:, :hidden_units]
    upward = gate_up[:, hidden_units:]
    return (gate, upward, jax.nn.sigmoid(gate))


def gate_backward(hidden_grad, gate, upward, sigma):
    return jnp.concatenate(
        [hidden_grad * upward * sigma * (1.0 + gate * (1.0 - sigma)), hidden_grad * gate * sigma],
        axis=1,
    ).astype(jnp.bfloat16)


def routed_body(tokens, expert_ids, scores, weight_in, weight_out, out_grad):
    n_data = lax.axis_size("dp")
    tok_count, slab_width = tokens.shape
    top_count = expert_ids.shape[1]
    hidden_units = weight_out.shape[1]
    capacity = min(tok_count, 5 * tok_count * top_count // (4 * n_data))
    routed = tok_count * top_count
    group_rows = n_data * capacity
    slot_count = n_data * capacity
    flat_ids = expert_ids.reshape(routed)
    expert_hot = (flat_ids[:, None] == jnp.arange(n_data, dtype=jnp.int32)[None, :]).astype(
        jnp.int32
    )
    place = jnp.arange(routed, dtype=jnp.int32)
    before = jnp.dot(
        (place[:, None] > place[None, :]).astype(jnp.bfloat16),
        expert_hot.astype(jnp.bfloat16),
        preferred_element_type=jnp.float32,
    ).astype(jnp.int32)
    earlier = jnp.sum(before * expert_hot, axis=1)
    target = flat_ids * capacity + earlier
    placing = (jnp.arange(slot_count, dtype=jnp.int32)[:, None] == target[None, :]).astype(
        jnp.bfloat16
    )
    token_place = jnp.sum(
        placing.reshape(slot_count, tok_count, top_count).astype(jnp.float32), axis=2
    ).astype(jnp.bfloat16)
    score_total = jnp.sum(scores, axis=1, keepdims=True)
    route_weights = ROUTE_SCALE * scores / score_total
    routed_grad = (route_weights[:, :, None] * out_grad.astype(jnp.float32)[:, None, :]).astype(
        jnp.bfloat16
    )
    routed_grad = routed_grad.reshape(routed, slab_width)
    token_send = jnp.dot(token_place, tokens, preferred_element_type=jnp.float32).astype(
        jnp.bfloat16
    )
    grad_send = jnp.dot(placing, routed_grad, preferred_element_type=jnp.float32).astype(
        jnp.bfloat16
    )
    token_slab, grad_slab = (
        lax.all_to_all(
            token_send.reshape(n_data, capacity, slab_width),
            "dp",
            split_axis=0,
            concat_axis=0,
            tiled=True,
        ),
        lax.all_to_all(
            grad_send.reshape(n_data, capacity, slab_width),
            "dp",
            split_axis=0,
            concat_axis=0,
            tiled=True,
        ),
    )
    token_slab = token_slab.reshape(group_rows, slab_width)
    grad_slab = grad_slab.reshape(group_rows, slab_width)
    in_slab = weight_in[0]
    out_slab = weight_out[0]
    gate_up_own = lax.psum_scatter(
        jnp.dot(token_slab, in_slab, preferred_element_type=jnp.float32),
        "expert",
        scatter_dimension=0,
        tiled=True,
    )
    gate_own, up_own, sig_own = gate_terms(gate_up_own, hidden_units)
    hidden_own = (gate_own * sig_own * up_own).astype(jnp.bfloat16)
    piece = lax.all_gather(hidden_own, "expert", axis=0, tiled=True)
    product = jnp.dot(piece, out_slab, preferred_element_type=jnp.float32)
    out_rows = product
    weight_sum = jnp.einsum("rf,rd->fd", piece, grad_slab, preferred_element_type=jnp.float32)
    out_rows, out_weight_sum = (out_rows, weight_sum)
    expert_out = out_rows.astype(jnp.bfloat16)
    out_blocks = expert_out.reshape(n_data, capacity, slab_width)
    out_back = lax.all_to_all(out_blocks, "dp", split_axis=0, concat_axis=0, tiled=True)
    hidden_grad = lax.psum_scatter(
        jnp.einsum("rd,fd->rf", grad_slab, out_slab, preferred_element_type=jnp.float32),
        "expert",
        scatter_dimension=0,
        tiled=True,
    )
    gate_up_grad = gate_backward(hidden_grad, gate_own, up_own, sig_own)
    piece = lax.all_gather(gate_up_grad, "expert", axis=0, tiled=True)
    product = jnp.einsum("rh,dh->rd", piece, in_slab, preferred_element_type=jnp.float32)
    input_rows = product
    weight_sum = jnp.einsum("rd,rh->dh", token_slab, piece, preferred_element_type=jnp.float32)
    input_rows, in_weight_sum = (input_rows, weight_sum)
    grad_blocks = input_rows.astype(jnp.bfloat16).reshape(n_data, capacity, slab_width)
    grad_back = lax.all_to_all(grad_blocks, "dp", split_axis=0, concat_axis=0, tiled=True)
    outputs_in = out_back.reshape(slot_count, slab_width)
    grads_in = grad_back.reshape(slot_count, slab_width)
    picked = jnp.einsum("sr,sd->rd", placing, outputs_in, preferred_element_type=jnp.float32)
    picked = picked.reshape(tok_count, top_count, slab_width)
    layer_out = jnp.sum(route_weights[:, :, None] * picked, axis=1).astype(jnp.bfloat16)
    partial_dot = jnp.sum(out_grad.astype(jnp.float32)[:, None, :] * picked, axis=2)
    choice_dot = lax.psum(partial_dot, "expert")
    scores_grad = (
        ROUTE_SCALE * choice_dot - jnp.sum(choice_dot * route_weights, axis=1, keepdims=True)
    ) / score_total
    tokens_grad = jnp.einsum(
        "st,sd->td", token_place, grads_in, preferred_element_type=jnp.float32
    ).astype(jnp.bfloat16)
    return (
        layer_out,
        tokens_grad,
        scores_grad,
        in_weight_sum.astype(jnp.bfloat16)[None],
        out_weight_sum.astype(jnp.bfloat16)[None],
    )


def swap(value, axis, bit):
    size = lax.axis_size(axis)
    return lax.ppermute(value, axis, [(i, i ^ bit) for i in range(size)])


def gather_line(block):
    size = lax.axis_size("dp")
    line = size // 2
    ahead, behind = [block], [block]
    for _ in range(line - 1):
        ahead.append(lax.ppermute(ahead[-1], "dp", [(i, i + 2) for i in range(size - 2)]))
        behind.append(lax.ppermute(behind[-1], "dp", [(i, i - 2) for i in range(2, size)]))
    near = [block] + [ahead[s] + behind[line - s] for s in range(1, line)]
    near = jnp.concatenate(near, axis=0)
    return jnp.concatenate([near, swap(near, "dp", 1)], axis=0)


def sum_parts(partial, high, low):
    rows, width = partial.shape
    quarters = partial.reshape(2, 2, rows // 4, width)
    kept = jnp.where(low == 0, quarters[:, 0], quarters[:, 1])
    given = jnp.where(low == 0, quarters[:, 1], quarters[:, 0])
    pair = kept + swap(given, "expert", 1)
    away = jnp.where(high == 0, pair[1], pair[0]).astype(jnp.bfloat16)
    home = jnp.where(high == 0, pair[0], pair[1])
    return home + swap(away, "expert", 2).astype(jnp.float32)


def join_parts(own, high, low):
    far = swap(own, "expert", 2)
    pair = jnp.stack([jnp.where(high == 0, own, far), jnp.where(high == 0, far, own)])
    other = swap(pair, "expert", 1)
    both = jnp.stack(
        [jnp.where(low == 0, pair, other), jnp.where(low == 0, other, pair)], axis=1
    )
    return both.reshape(4 * own.shape[0], own.shape[1])


def from_offsets(blocks):
    size = lax.axis_size("dp")
    line = size // 2
    arrived = [blocks[0]]
    for r in range(1, size):
        across, step = r // line, r % line
        pairs = [(i, ((i // 2 - step) % line) * 2 + ((i % 2) ^ across)) for i in range(size)]
        arrived.append(lax.ppermute(blocks[r], "dp", pairs))
    return arrived


def send_home(blocks):
    total = blocks[0].astype(jnp.float32)
    for arrived in from_offsets(blocks)[1:]:
        total = total + arrived.astype(jnp.float32)
    return total.astype(jnp.bfloat16)


def dense_body(tokens, expert_ids, scores, weight_in, weight_out, out_grad):
    n_data = lax.axis_size("dp")
    line = n_data // 2
    tok_count, slab_width = tokens.shape
    hidden_units = weight_out.shape[1]
    rows = n_data * tok_count
    own_rows = rows // 4
    mine, part = lax.axis_index("dp"), lax.axis_index("expert")
    high, low = part // 2, part % 2
    in_slab = weight_in[0]
    out_slab = weight_out[0]
    score_total = jnp.sum(scores, axis=1, keepdims=True)
    route_weights = ROUTE_SCALE * scores / score_total
    experts = jnp.arange(n_data, dtype=jnp.int32)
    chosen = expert_ids[:, :, None] == experts[None, None, :]
    by_expert = jnp.sum(jnp.where(chosen, route_weights[:, :, None], 0.0), axis=1)
    all_weights = gather_line(by_expert.T)
    mine_weights = all_weights.reshape(n_data, n_data, tok_count)
    mine_weights = jnp.sum(jnp.where((experts == mine)[None, :, None], mine_weights, 0.0), axis=1)
    own_weight = mine_weights.reshape(4, own_rows)
    own_weight = jnp.take(own_weight, part, axis=0)[:, None]
    token_slab = gather_line(tokens)
    grad_slab = gather_line(out_grad)
    gate_up_own = sum_parts(
        jnp.dot(token_slab, in_slab, preferred_element_type=jnp.float32), high, low
    )
    raw_own = sum_parts(
        jnp.einsum("rd,fd->rf", grad_slab, out_slab, preferred_element_type=jnp.float32), high, low
    )
    gate, upward, sigma = gate_terms(gate_up_own, hidden_units)
    hidden = gate * sigma * upward
    hidden_all = join_parts((own_weight * hidden).astype(jnp.bfloat16), high, low)
    gug_all = join_parts(gate_backward(own_weight * raw_own, gate, upward, sigma), high, low)
    dot_own = jnp.sum(hidden * raw_own, axis=1)
    dot_home = jnp.stack(from_offsets(join_parts(dot_own.reshape(-1, tok_count), high, low)))
    offset = ((experts % 2) ^ (mine % 2)) * line + (experts // 2 - mine // 2) % line
    at_offset = offset[:, None] == experts[None, :]
    dot_by_expert = jnp.sum(jnp.where(at_offset[:, :, None], dot_home[None], 0.0), axis=1)
    choice_dot = jnp.sum(jnp.where(chosen, dot_by_expert.T[:, None, :], 0.0), axis=2)
    scores_grad = (
        ROUTE_SCALE * choice_dot - jnp.sum(choice_dot * route_weights, axis=1, keepdims=True)
    ) / score_total
    out_rows = jnp.dot(hidden_all, out_slab, preferred_element_type=jnp.float32)
    layer_out = send_home(out_rows.astype(jnp.bfloat16).reshape(n_data, tok_count, slab_width))
    in_rows = jnp.einsum("rh,dh->rd", gug_all, in_slab, preferred_element_type=jnp.float32)
    tokens_grad = send_home(in_rows.astype(jnp.bfloat16).reshape(n_data, tok_count, slab_width))
    out_weight = jnp.einsum("rf,rd->fd", hidden_all, grad_slab, preferred_element_type=jnp.float32)
    in_weight = jnp.einsum("rd,rh->dh", token_slab, gug_all, preferred_element_type=jnp.float32)
    return (
        layer_out,
        tokens_grad,
        scores_grad,
        in_weight.astype(jnp.bfloat16)[None],
        out_weight.astype(jnp.bfloat16)[None],
    )


def body(tokens, expert_ids, *rest):
    n_data, n_part = lax.axis_size("dp"), lax.axis_size("expert")
    dense = expert_ids.shape[1] == n_data and n_data % 4 == 0 and n_part == 4
    return (dense_body if dense else routed_body)(tokens, expert_ids, *rest)


def solution(mesh):
    placed = (
        P("dp", "expert"),
        P("dp", None),
        P("dp", None),
        P("dp", "expert", None),
        P("dp", None, "expert"),
        P("dp", "expert"),
    )
    return jax.shard_map(
        body,
        mesh=mesh,
        in_specs=placed,
        out_specs=(
            P("dp", "expert"),
            P("dp", "expert"),
            P("dp", None),
            P("dp", "expert", None),
            P("dp", None, "expert"),
        ),
        check_vma=False,
    )
```
